32 devices in a mesh: dp: 8 (over z, x), ctx: 4 (over y, core).
Axes of the slice: x: 2, y: 2, z: 4, core: 2. Of those that a mesh axis runs over, the one named last changes fastest.
Arguments:
- tokens: bfloat16 [8, 2048, 576], P('dp', 'ctx'), may hold values from -6 to 6
- cotangent: bfloat16 [8, 2048, 576], P('dp', 'ctx'), may hold values from -6 to 6
- positions: int32 [8, 2048], P('dp', 'ctx'), may hold values from 0 to 4094, as said below
- block_order: int32 [4], replicated, may hold values from 0 to 3, as said below
- norm_gains: bfloat16 [2, 576], P(None, 'dp'), may hold values from 0.5 to 1.5
- w_query: bfloat16 [576, 576], P('dp', 'ctx'), may hold values from -0.4375 to 0.4375
- w_key: bfloat16 [576, 192], P('dp', 'ctx'), may hold values from -0.25 to 0.25
- w_value: bfloat16 [576, 192], P('dp', 'ctx'), may hold values from -0.25 to 0.25
- w_output: bfloat16 [576, 576], P('dp', 'ctx'), may hold values from -1.5 to 1.5
- w_gate: bfloat16 [576, 1536], P('dp', 'ctx'), may hold values from -0.25 to 0.25
- w_up: bfloat16 [576, 1536], P('dp', 'ctx'), may hold values from -0.25 to 0.25
- w_down: bfloat16 [1536, 576], P('dp', 'ctx'), may hold values from -0.15625 to 0.15625
Outputs:
- outputs: bfloat16 [8, 2048, 576], P('dp', 'ctx')
- input_grad: bfloat16 [8, 2048, 576], P('dp', 'ctx')
- grad_gains: float32 [2, 576], P(None, 'dp')
- grad_query: float32 [576, 576], P('dp', 'ctx')
- grad_key: float32 [576, 192], P('dp', 'ctx')
- grad_value: float32 [576, 192], P('dp', 'ctx')
- grad_output: float32 [576, 576], P('dp', 'ctx')
- grad_gate: float32 [576, 1536], P('dp', 'ctx')
- grad_up: float32 [576, 1536], P('dp', 'ctx')
- grad_down: float32 [1536, 576], P('dp', 'ctx')
The draws below stay inside these ranges and needn't reach their ends.
Inputs may be any that keep to these rules, and one draw needn't show every extreme that they name: A permutation: the ctx device of index c holds block block_order[c] of each sequence's causal order. Along the causal order of a sequence the positions start at 0, rise by 1 to 3 from token to token, and end at 4094.
All inputs are finite; a program needn't handle non-finite values.
Results may differ from the reference program's by a relative error of at most 0.022.
Values may be sent and summed in bfloat16 or wider, within the bound.
A program may use at most 128 MiB of HBM per device.

```python
import math
import jax
import jax.numpy as jnp
from jax import lax

D = 576
FF = 1536
HEADS = 9
KV_HEADS = 3
HEAD = 64
TOK_DEV = 512
SEQ = 2048
SEQS = 8


def block_permutation(key):
    return jax.random.permutation(jax.random.fold_in(key, 11), SEQ // TOK_DEV).astype(jnp.int32)


def draw_block_order(key, part):
    order = block_permutation(key)
    return order


def draw_positions(key, part):
    order = block_permutation(key)
    key = jax.random.fold_in(key, 5)
    firsts = jax.random.randint(key, (SEQS, (SEQ - 2) // 2), 1, 4, dtype=jnp.int32)
    paired = jnp.stack([firsts, 4 - firsts], axis=-1).reshape(SEQS, SEQ - 2)
    steps = jnp.concatenate([jnp.zeros((SEQS, 1), jnp.int32), paired, jnp.full((SEQS, 1), 2, jnp.int32)], axis=1)
    running = jnp.cumsum(steps, axis=1).astype(jnp.int32)
    places = jnp.arange(SEQ, dtype=jnp.int32)
    ranks = order[places // TOK_DEV] * TOK_DEV + places % TOK_DEV
    return jnp.take(running, ranks, axis=1).astype(jnp.int32)


def levels(own_key, shape, shards, low, top_value):
    def one(position, blocks):
        heights = jax.random.uniform(jax.random.fold_in(jax.random.fold_in(own_key, 6), position), (blocks,), jnp.float32, low / len(shards), top_value / len(shards))
        return jnp.repeat(jnp.exp(heights), shape[position] // blocks).reshape((-1,) + (1,) * (len(shape) - position - 1))

    loudness = one(*shards[0])
    for cut in shards[1:]:
        loudness = loudness * one(*cut)
    return loudness


def centred(own_key, extent, scale, bound, shards=(), kind=jnp.bfloat16):
    array = jax.random.normal(own_key, extent, jnp.float32) * scale
    if len(shards) > 0:
        array = levels(own_key, extent, shards, -0.22, 0.18) * array
    return jnp.clip(array, min=-bound, max=bound).astype(kind)


def setup_inputs(seed: int = 0) -> dict:
    arg_keys = jax.random.split(jax.random.key(seed), 13)
    tokens = centred(arg_keys[0], (SEQS, SEQ, D), 1.0, 6.0, ((0, 8), (1, 4)))
    cotangent = centred(arg_keys[1], (SEQS, SEQ, D), 1.0, 6.0, ((0, 8), (1, 4)))
    positions = draw_positions(jax.random.fold_in(arg_keys[12], 71), 0)
    block_order = draw_block_order(jax.random.fold_in(arg_keys[12], 71), 0)
    norm_gains = jnp.clip(1.0 + 0.1 * jax.random.normal(arg_keys[4], (2, D), jnp.float32), 0.5, 1.5).astype(jnp.bfloat16)
    w_query = centred(arg_keys[5], (D, D), (D // 3) ** -0.5, 0.4375, ((0, 8), (1, 4)))
    w_key = centred(arg_keys[6], (D, KV_HEADS * HEAD), D ** -0.5, 0.25, ((0, 8), (1, 4)))
    w_value = centred(arg_keys[7], (D, KV_HEADS * HEAD), D ** -0.5, 0.25, ((0, 8), (1, 4)))
    w_output = centred(arg_keys[8], (D, D), (D // 32) ** -0.5, 1.5, ((0, 8), (1, 4)))
    w_gate = centred(arg_keys[9], (D, FF), D ** -0.5, 0.25, ((0, 8), (1, 4)))
    w_up = centred(arg_keys[10], (D, FF), D ** -0.5, 0.25, ((0, 8), (1, 4)))
    w_down = centred(arg_keys[11], (FF, D), FF ** -0.5, 0.15625, ((0, 8), (1, 4)))
    return {"tokens": tokens, "cotangent": cotangent, "positions": positions, "block_order": block_order, "norm_gains": norm_gains, "w_query": w_query, "w_key": w_key, "w_value": w_value, "w_output": w_output, "w_gate": w_gate, "w_up": w_up, "w_down": w_down}


norm_eps = 1e-05
rope_base = 100000.0
masked_score = -1e+30
highest = lax.Precision.HIGHEST

@jax.custom_vjp
def low(v):
    return lax.optimization_barrier(v.astype(jnp.bfloat16)).astype(jnp.float32)

@jax.custom_vjp
def low_back(v):
    return v

def low_keep(v):
    return (low(v), None)

def low_pass(kept, grad):
    return (grad,)

def back_keep(v):
    return (v, None)

def back_low(kept, grad):
    return (low(grad),)
low.defvjp(low_keep, low_pass)
low_back.defvjp(back_keep, back_low)

def normalize(values, gain):
    inverse_rms = lax.rsqrt(lax.optimization_barrier(jnp.mean(values * values, axis=-1, keepdims=True)) + norm_eps)
    return values * inverse_rms * gain

def angles_for(positions):
    half_width = HEAD // 2
    inverse = rope_base ** (-(jnp.arange(half_width, dtype=jnp.float32) * 2.0) / HEAD)
    turned = positions.astype(jnp.float32)[:, None] * inverse[None, :]
    return (jnp.cos(turned), jnp.sin(turned))

def rotate(values, cos_part, sin_part, heads):
    shaped = values.reshape(values.shape[0], heads, HEAD)
    front_half = shaped[..., :HEAD // 2]
    back_half = shaped[..., HEAD // 2:]
    cosine_rows = cos_part[:, None, :]
    sine_rows = sin_part[:, None, :]
    turned = jnp.concatenate([front_half * cosine_rows - back_half * sine_rows, back_half * cosine_rows + front_half * sine_rows], axis=-1)
    return turned.reshape(values.shape)

def attention(query, keys, values, ranks):
    length = query.shape[0]
    size = math.gcd(length, 512)
    groups = HEADS // KV_HEADS
    key_heads = keys.reshape(length, KV_HEADS, HEAD)
    value_heads = values.reshape(length, KV_HEADS, HEAD)

    def one_block(inputs):
        block_query, block_ranks = inputs
        raw = jnp.einsum('qgrd,kgd->grqk', block_query, key_heads, precision=highest)
        scores = low_back(raw * (1.0 / math.sqrt(HEAD)))
        allowed = ranks[None, None, None, :] <= block_ranks[None, None, :, None]
        scores = jnp.where(allowed, scores, masked_score)
        top = lax.optimization_barrier(jnp.max(scores, axis=-1, keepdims=True))
        expo = jnp.exp(scores - top)
        probs = low(expo / lax.optimization_barrier(jnp.sum(expo, axis=-1, keepdims=True)))
        return jnp.einsum('grqk,kgd->qgrd', probs, value_heads, precision=highest)
    blocks = (query.reshape(length // size, size, KV_HEADS, groups, HEAD), ranks.reshape(length // size, size))
    mixed = lax.map(jax.checkpoint(one_block), blocks)
    return mixed.reshape(length, HEADS * HEAD)

def layer(x_rows, gains, w_query, w_key, w_value, w_output, w_gate, w_up, w_down, cos_part, sin_part, ranks):
    act_one = low(normalize(x_rows, gains[0]))
    query = low(rotate(low_back(jnp.dot(act_one, w_query, precision=highest)), cos_part, sin_part, HEADS))
    keys = low(rotate(low_back(jnp.dot(act_one, w_key, precision=highest)), cos_part, sin_part, KV_HEADS))
    values = low_back(low(jnp.dot(act_one, w_value, precision=highest)))
    mixed = low_back(low(attention(query, keys, values, ranks)))
    resid = x_rows + low_back(jnp.dot(mixed, w_output, precision=highest))
    act_two = low(normalize(resid, gains[1]))
    gate = low_back(jnp.dot(act_two, w_gate, precision=highest))
    upper = low_back(jnp.dot(act_two, w_up, precision=highest))
    hidden = low(gate * jax.nn.sigmoid(gate) * upper)
    return resid + low_back(jnp.dot(hidden, w_down, precision=highest))

def reference(tokens, cotangent, positions, block_order, norm_gains, w_query, w_key, w_value, w_output, w_gate, w_up, w_down):
    params = (norm_gains.astype(jnp.float32), w_query.astype(jnp.float32), w_key.astype(jnp.float32), w_value.astype(jnp.float32), w_output.astype(jnp.float32), w_gate.astype(jnp.float32), w_up.astype(jnp.float32), w_down.astype(jnp.float32))
    order_rank = (block_order[:, None] * TOK_DEV + jnp.arange(TOK_DEV, dtype=jnp.int32)[None, :]).reshape(-1).astype(jnp.int32)

    def one_sequence(totals, inputs):
        x_seq, grad_seq, where = inputs
        cos_part, sin_part = angles_for(where)

        def forward(x_rows, weights):
            return layer(x_rows, *weights, cos_part, sin_part, order_rank)
        result, pull = jax.vjp(forward, x_seq.astype(jnp.float32), params)
        grad_x, grad_params = pull(grad_seq.astype(jnp.float32))
        totals = jax.tree.map(lambda left, right: left + right, totals, grad_params)
        return (totals, (result.astype(jnp.bfloat16), grad_x.astype(jnp.bfloat16)))
    zeros = tuple((jnp.zeros(param.shape, jnp.float32) for param in params))
    totals, stacked = lax.scan(one_sequence, zeros, (tokens, cotangent, positions))
    return (stacked[0], stacked[1], totals[0], totals[1], totals[2], totals[3], totals[4], totals[5], totals[6], totals[7])
```

```python
import functools
import math

import jax
import jax.numpy as jnp
from jax import lax
from jax.experimental import pallas as pl
from jax.experimental.pallas import tpu as pltpu
from jax.sharding import PartitionSpec as P

HEADS = 9
KV_HEADS = 3
HEAD = 64


norm_eps = 1e-05
rope_base = 100000.0
masked_score = -1e30


def normalize(values, gain):
    inverse_rms = lax.rsqrt(jnp.mean(values * values, axis=-1, keepdims=True) + norm_eps)
    unit_rows = values * inverse_rms
    return (unit_rows * gain, unit_rows, inverse_rms)


def norm_back(grad, unit_rows, inverse_rms, gain):
    grad_unit = grad * gain
    inner = jnp.mean(grad_unit * unit_rows, axis=-1, keepdims=True)
    return (inverse_rms * (grad_unit - unit_rows * inner), jnp.sum(grad * unit_rows, axis=0))


def angles_for(positions):
    half_width = HEAD // 2
    inverse = rope_base ** (-(jnp.arange(half_width, dtype=jnp.float32) * 2.0) / HEAD)
    turned = positions.astype(jnp.float32)[:, None] * inverse[None, :]
    return (jnp.cos(turned), jnp.sin(turned))


def rotate(values, cos_part, sin_part, heads):
    shaped = values.reshape(values.shape[0], heads, HEAD)
    front_half = shaped[..., : HEAD // 2]
    back_half = shaped[..., HEAD // 2 :]
    cosine_rows = cos_part[:, None, :]
    sine_rows = sin_part[:, None, :]
    turned = jnp.concatenate(
        [
            front_half * cosine_rows - back_half * sine_rows,
            back_half * cosine_rows + front_half * sine_rows,
        ],
        axis=-1,
    )
    return turned.reshape(values.shape)


def block_scores(query, keys, query_ranks, key_ranks):
    raw = jnp.einsum("qgrd,kgd->grqk", query, keys, preferred_element_type=jnp.float32) * (
        1.0 / math.sqrt(HEAD)
    )
    allowed = key_ranks[None, None, None, :] <= query_ranks[None, None, :, None]
    return jnp.where(allowed, raw, masked_score)


def split_keys(keys, values, key_ranks):
    size = math.gcd(keys.shape[0], 1024)
    count = keys.shape[0] // size
    return (
        keys.reshape(count, size, KV_HEADS, HEAD),
        values.reshape(count, size, KV_HEADS, HEAD),
        key_ranks.reshape(count, size),
    )


def attend_forward(query, keys, values, query_ranks, key_ranks):
    rows = query.shape[0]
    count = rows // rows
    groups = HEADS // KV_HEADS
    key_parts = split_keys(keys, values, key_ranks)

    def one_block(inputs):
        block_query, block_ranks = inputs

        def running(carry, part):
            top, total = carry
            scores = block_scores(block_query, part[0], block_ranks, part[2])
            new_top = jnp.maximum(top, jnp.max(scores, axis=-1))
            total = total * jnp.exp(top - new_top) + jnp.sum(
                jnp.exp(scores - new_top[..., None]), axis=-1
            )
            return ((new_top, total), None)

        start = jnp.full((KV_HEADS, groups, rows), masked_score, jnp.float32)
        (top, total), unused = lax.scan(running, (start, jnp.zeros_like(start)), key_parts)
        log_total = top + jnp.log(total)

        def mixing(acc, part):
            scores = block_scores(block_query, part[0], block_ranks, part[2])
            weights = jnp.exp(scores - log_total[..., None]).astype(jnp.bfloat16)
            return (
                acc
                + jnp.einsum(
                    "grqk,kgd->qgrd", weights, part[1], preferred_element_type=jnp.float32
                ),
                None,
            )

        mixed, unused = lax.scan(
            mixing, jnp.zeros((rows, KV_HEADS, groups, HEAD), jnp.float32), key_parts
        )
        return (mixed, log_total)

    blocks = (query.reshape(count, rows, KV_HEADS, groups, HEAD), query_ranks.reshape(count, rows))
    mixed, log_total = lax.map(one_block, blocks)
    return (mixed, log_total)


def attend_backward(query, keys, values, query_ranks, key_ranks, mixed, log_total, grad_mixed):
    rows = query.shape[0]
    count = rows // rows
    groups = HEADS // KV_HEADS
    scale = 1.0 / math.sqrt(HEAD)
    key_parts = split_keys(keys, values, key_ranks)

    def one_block(carry, inputs):
        block_query, block_ranks, block_grad, block_mixed, block_log = inputs
        block_inner = jnp.transpose(
            jnp.sum(block_grad.astype(jnp.float32) * block_mixed, axis=-1), (1, 2, 0)
        )

        def per_keys(grad_query, part):
            keys_part, values_part, ranks_part = part
            scores = block_scores(block_query, keys_part, block_ranks, ranks_part)
            probs = jnp.exp(scores - block_log[..., None])
            grad_probs = jnp.einsum(
                "qgrd,kgd->grqk", block_grad, values_part, preferred_element_type=jnp.float32
            )
            grad_scores = (probs * (grad_probs - block_inner[..., None])).astype(jnp.bfloat16)
            grad_query = (
                grad_query
                + jnp.einsum(
                    "grqk,kgd->qgrd", grad_scores, keys_part, preferred_element_type=jnp.float32
                )
                * scale
            )
            grad_keys = (
                jnp.einsum(
                    "grqk,qgrd->kgd", grad_scores, block_query, preferred_element_type=jnp.float32
                )
                * scale
            )
            grad_values = jnp.einsum(
                "grqk,qgrd->kgd",
                probs.astype(jnp.bfloat16),
                block_grad,
                preferred_element_type=jnp.float32,
            )
            return (grad_query, (grad_keys, grad_values))

        start = jnp.zeros((rows, KV_HEADS, groups, HEAD), jnp.float32)
        grad_query, pieces = lax.scan(per_keys, start, key_parts)
        total_keys, total_values = carry
        total_keys = total_keys + pieces[0].reshape(total_keys.shape)
        total_values = total_values + pieces[1].reshape(total_values.shape)
        return ((total_keys, total_values), grad_query)

    empty = jnp.zeros((keys.shape[0], KV_HEADS * HEAD), jnp.float32)
    blocks = (
        query.reshape(count, rows, KV_HEADS, groups, HEAD),
        query_ranks.reshape(count, rows),
        grad_mixed.reshape(count, rows, KV_HEADS, groups, HEAD),
        mixed,
        log_total,
    )
    (grad_keys, grad_values), grad_query = lax.scan(one_block, (empty, empty), blocks)
    return (grad_query.reshape(rows, HEADS * HEAD), grad_keys, grad_values)


def bit_orders(bits, slices):
    rest = list(bits[1:])
    orders = [
        [bits[0]] + rest,
        [bits[0]] + rest[2:] + rest[:2],
        [bits[0]] + rest[:2][::-1] + rest[2:],
    ]
    return [orders[s % 3] for s in range(slices)]


def bit_values(bits):
    ctx_bits = lax.axis_size("ctx").bit_length() - 1
    dp_index, ctx_index = lax.axis_index("dp"), lax.axis_index("ctx")
    values = {}
    partners = {}
    for bit in bits:
        if bit < ctx_bits:
            step = 1 << bit
            value = lax.rem(ctx_index // step, 2)
            partners[bit] = (dp_index, ctx_index + step * (1 - 2 * value))
        else:
            step = 1 << (bit - ctx_bits)
            value = lax.rem(dp_index // step, 2)
            partners[bit] = (dp_index + step * (1 - 2 * value), ctx_index)
        values[bit] = value
    return values, partners


def greet(partners):
    barrier = pltpu.get_barrier_semaphore()
    for partner in partners.values():
        pl.semaphore_signal(
            barrier, inc=1, device_id=partner, device_id_type=pl.DeviceIdType.MESH
        )
    pl.semaphore_wait(barrier, len(partners))


def gather_body(bits, orders, in_refs, out_refs, local_sem, send_sem, recv_sem):
    values, partners = bit_values(bits)
    stages = len(bits)
    linear = []
    for order in orders:
        total = 0
        for place, bit in enumerate(order):
            total = total + values[bit] * (1 << (stages - 1 - place))
        linear.append(total)
    local = [
        pltpu.make_async_copy(in_refs[s], out_refs[s].at[linear[s]], local_sem.at[s])
        for s in range(len(orders))
    ]
    for copy in local:
        copy.start()
    greet(partners)
    for copy in local:
        copy.wait()
    copies = {}
    for stage in range(stages):
        count = 1 << stage
        for s, order in enumerate(orders):
            if stage > 0:
                copies[s, stage - 1].wait_recv()
            part = out_refs[s].at[pl.ds((linear[s] // count) * count, count)]
            copies[s, stage] = pltpu.make_async_remote_copy(
                src_ref=part,
                dst_ref=part,
                send_sem=send_sem.at[s, stage],
                recv_sem=recv_sem.at[s, stage],
                device_id=partners[order[stages - 1 - stage]],
                device_id_type=pl.DeviceIdType.MESH,
            )
            copies[s, stage].start()
    for s in range(len(orders)):
        copies[s, stages - 1].wait_recv()
        for stage in range(stages):
            copies[s, stage].wait_send()


def gather_kernel(bits, orders, *refs):
    count = len(orders)
    gather_body(bits, orders, refs[:count], refs[count : 2 * count], *refs[2 * count :])


def comm_params(ident, need):
    return pltpu.CompilerParams(
        collective_id=ident, has_side_effects=True, vmem_limit_bytes=need
    )


def standard(order, bits):
    return [order.index(bit) for bit in bits[::-1]]


def gather_all(parts, bits, ident):
    orders = bit_orders(bits, len(parts))
    stages = len(bits)
    total = 1 << stages
    outs = pl.pallas_call(
        functools.partial(gather_kernel, bits, orders),
        out_shape=[jax.ShapeDtypeStruct((total,) + p.shape, p.dtype) for p in parts],
        in_specs=[pl.BlockSpec(memory_space=pltpu.VMEM)] * len(parts),
        out_specs=[pl.BlockSpec(memory_space=pltpu.VMEM)] * len(parts),
        scratch_shapes=[
            pltpu.SemaphoreType.DMA((len(parts),)),
            pltpu.SemaphoreType.DMA((len(parts), stages)),
            pltpu.SemaphoreType.DMA((len(parts), stages)),
        ],
        compiler_params=comm_params(ident, 40 << 20),
    )(*parts)
    results = []
    for out, order in zip(outs, orders):
        shape = out.shape[1:]
        spread = out.reshape((2,) * stages + shape)
        perm = standard(order, bits) + [stages, stages + 1]
        results.append(jnp.transpose(spread, perm).reshape((total,) + shape))
    return results


def reduce_kernel(bits, orders, *refs):
    slices = len(orders)
    stages = len(bits)
    in_refs, out_refs = refs[:slices], refs[slices : 2 * slices]
    recv = refs[2 * slices : 2 * slices + slices * stages]
    work = refs[2 * slices + slices * stages : 2 * slices + slices * (2 * stages - 1)]
    send_sem, recv_sem = refs[-2], refs[-1]
    values, partners = bit_values(bits)
    greet(partners)
    copies = {}
    for stage in range(stages + 1):
        for s, order in enumerate(orders):
            if stage > 0:
                past = stage - 1
                half = 1 << (stages - 1 - past)
                source = in_refs[s] if past == 0 else work[s * (stages - 1) + past - 1]
                arrived = recv[s * stages + past]
                own = values[order[past]] * half
                copies[s, past].wait_recv()
                last = past == stages - 1

                def add(k, unused, source=source, arrived=arrived, own=own, last=last, s=s, past=past):
                    total = source[own + k].astype(jnp.float32) + arrived[k].astype(jnp.float32)
                    if last:
                        out_refs[s][...] = total
                    else:
                        work[s * (stages - 1) + past][k] = total.astype(jnp.bfloat16)
                    return unused

                if last:
                    add(0, 0)
                else:
                    lax.fori_loop(0, half, add, 0)
            if stage < stages:
                half = 1 << (stages - 1 - stage)
                source = in_refs[s] if stage == 0 else work[s * (stages - 1) + stage - 1]
                other = (1 - values[order[stage]]) * half
                copies[s, stage] = pltpu.make_async_remote_copy(
                    src_ref=source.at[pl.ds(other, half)],
                    dst_ref=recv[s * stages + stage],
                    send_sem=send_sem.at[s, stage],
                    recv_sem=recv_sem.at[s, stage],
                    device_id=partners[order[stage]],
                    device_id_type=pl.DeviceIdType.MESH,
                )
                copies[s, stage].start()
    for copy in copies.values():
        copy.wait_send()


def reduce_all(parts, bits, ident):
    orders = bit_orders(bits, len(parts))
    stages = len(bits)
    total = 1 << stages
    ready = []
    for part, order in zip(parts, orders):
        shape = part.shape[1:]
        spread = part.reshape((2,) * stages + shape)
        perm = [stages - 1 - bits.index(bit) for bit in order] + [stages, stages + 1]
        ready.append(jnp.transpose(spread, perm).reshape((total,) + shape))
    recv = [
        pltpu.VMEM((1 << (stages - 1 - t),) + p.shape[1:], jnp.bfloat16)
        for p in parts
        for t in range(stages)
    ]
    work = [
        pltpu.VMEM((1 << (stages - 1 - t),) + p.shape[1:], jnp.bfloat16)
        for p in parts
        for t in range(stages - 1)
    ]
    return pl.pallas_call(
        functools.partial(reduce_kernel, bits, orders),
        out_shape=[jax.ShapeDtypeStruct(p.shape[1:], jnp.float32) for p in parts],
        in_specs=[pl.BlockSpec(memory_space=pltpu.VMEM)] * len(parts),
        out_specs=[pl.BlockSpec(memory_space=pltpu.VMEM)] * len(parts),
        scratch_shapes=recv
        + work
        + [
            pltpu.SemaphoreType.DMA((len(parts), stages)),
            pltpu.SemaphoreType.DMA((len(parts), stages)),
        ],
        compiler_params=comm_params(ident, 56 << 20),
    )(*ready)


def pad_rows(block, rows):
    return jnp.pad(block, ((0, 0),) * (block.ndim - 2) + ((0, rows - block.shape[-2]), (0, 0)))


def thirds(block):
    size = block.shape[-1] // 3
    return [block[..., s * size : (s + 1) * size] for s in range(3)]


def per_device(
    tokens,
    cotangent,
    positions,
    block_order,
    norm_gains,
    w_query,
    w_key,
    w_value,
    w_output,
    w_gate,
    w_up,
    w_down,
):
    ctx_count = lax.axis_size("ctx")
    dp_count = lax.axis_size("dp")
    ctx_bits = list(range(ctx_count.bit_length() - 1))
    all_bits = list(range((ctx_count * dp_count).bit_length() - 1))
    depth = w_query.shape[0]
    spans = [w.shape[1] for w in (w_query, w_key, w_value, w_output)]
    width = sum(spans)
    fold = w_down.shape[1] // depth
    early_rows = -(-(depth + 2) // 16) * 16
    late_rows = -(-depth // 16) * 16
    gain_rows = jnp.pad(norm_gains, ((0, early_rows - depth - 2), (0, width - depth)))
    early = jnp.concatenate(
        [jnp.concatenate([w_query, w_key, w_value, w_output], axis=1), gain_rows], axis=0
    )
    down_folded = (
        w_down.T.reshape(fold, depth, w_down.shape[0]).transpose(1, 0, 2).reshape(depth, width)
    )
    early_all = jnp.concatenate(gather_all(thirds(early), all_bits, 0), axis=-1)
    gate_all, up_all, down_all = gather_all(
        [pad_rows(w, late_rows) for w in (w_gate, w_up, down_folded)], all_bits, 1
    )
    early_all = early_all.reshape(dp_count, ctx_count, early_rows, width)

    def join_columns(blocks):
        return jnp.transpose(blocks, (0, 2, 1, 3)).reshape(dp_count * depth, -1)

    offsets = [sum(spans[:n]) for n in range(5)]
    full_query, full_key, full_value, full_output = (
        join_columns(early_all[:, :, :depth, offsets[n] : offsets[n + 1]]) for n in range(4)
    )
    gains_all = jnp.transpose(early_all[:, 0, depth : depth + 2, :depth], (1, 0, 2)).reshape(2, -1)

    def late_blocks(blocks):
        return blocks.reshape(dp_count, ctx_count, late_rows, width)[:, :, :depth]

    full_gate = join_columns(late_blocks(gate_all))
    full_up = join_columns(late_blocks(up_all))
    down_turned = (
        late_blocks(down_all)
        .reshape(dp_count, ctx_count, depth, fold, -1)
        .transpose(1, 3, 2, 0, 4)
        .reshape(ctx_count * fold * depth, -1)
    )
    rows = tokens.shape[1]
    device_index = lax.axis_index("ctx")
    row_index = jnp.arange(rows, dtype=jnp.int32)
    own_ranks = block_order[device_index] * rows + row_index
    key_ranks = (block_order[:, None] * rows + row_index[None, :]).reshape(-1)
    x_rows = tokens[0].astype(jnp.float32)
    grad_out = cotangent[0].astype(jnp.float32)
    cos_part, sin_part = angles_for(positions[0])
    gain_one = gains_all[0].astype(jnp.float32)
    gain_two = gains_all[1].astype(jnp.float32)
    normed_one, unit_one, inverse_one = normalize(x_rows, gain_one)
    act_one = normed_one.astype(jnp.bfloat16)
    query = rotate(
        jnp.dot(act_one, full_query, preferred_element_type=jnp.float32), cos_part, sin_part, HEADS
    ).astype(jnp.bfloat16)
    keys_local = rotate(
        jnp.dot(act_one, full_key, preferred_element_type=jnp.float32), cos_part, sin_part, KV_HEADS
    ).astype(jnp.bfloat16)
    values_local = jnp.dot(act_one, full_value, preferred_element_type=jnp.float32).astype(
        jnp.bfloat16
    )
    kv_width = KV_HEADS * HEAD
    pairs = gather_all(thirds(jnp.concatenate([keys_local, values_local], axis=1)), ctx_bits, 2)
    pairs = jnp.concatenate(pairs, axis=-1).reshape(ctx_count * rows, 2 * kv_width)
    keys_all, values_all = pairs[:, :kv_width], pairs[:, kv_width:]
    groups = HEADS // KV_HEADS
    query_heads = query.reshape(rows, KV_HEADS, groups, HEAD)
    mixed, log_total = attend_forward(query_heads, keys_all, values_all, own_ranks, key_ranks)
    mixed_rows = mixed.reshape(rows, HEADS * HEAD).astype(jnp.bfloat16)
    resid = x_rows + jnp.dot(mixed_rows, full_output, preferred_element_type=jnp.float32)
    normed_two, unit_two, inverse_two = normalize(resid, gain_two)
    act_two = normed_two.astype(jnp.bfloat16)
    gate = jnp.dot(act_two, full_gate, preferred_element_type=jnp.float32)
    upper = jnp.dot(act_two, full_up, preferred_element_type=jnp.float32)
    sigma = jax.nn.sigmoid(gate)
    hidden = (gate * sigma * upper).astype(jnp.bfloat16)
    result = resid + jnp.einsum(
        "tf,df->td", hidden, down_turned, preferred_element_type=jnp.float32
    )
    outputs = result.astype(jnp.bfloat16)[None]
    grad_branch = grad_out.astype(jnp.bfloat16)
    grad_down = jnp.einsum("td,tf->df", grad_branch, hidden, preferred_element_type=jnp.float32)
    grad_hidden = jnp.einsum(
        "td,df->tf", grad_branch, down_turned, preferred_element_type=jnp.float32
    )
    grad_gate_rows = (grad_hidden * upper * sigma * (1.0 + gate * (1.0 - sigma))).astype(
        jnp.bfloat16
    )
    grad_up_rows = (grad_hidden * gate * sigma).astype(jnp.bfloat16)
    grad_gate = jnp.einsum("td,tf->df", act_two, grad_gate_rows, preferred_element_type=jnp.float32)
    grad_up = jnp.einsum("td,tf->df", act_two, grad_up_rows, preferred_element_type=jnp.float32)
    grad_act_two = jnp.einsum(
        "tf,df->td", grad_gate_rows, full_gate, preferred_element_type=jnp.float32
    ) + jnp.einsum("tf,df->td", grad_up_rows, full_up, preferred_element_type=jnp.float32)
    grad_resid_norm, grad_gain_two = norm_back(grad_act_two, unit_two, inverse_two, gain_two)
    grad_resid = grad_out + grad_resid_norm
    grad_attn = grad_resid.astype(jnp.bfloat16)
    grad_output = jnp.einsum("te,td->ed", mixed_rows, grad_attn, preferred_element_type=jnp.float32)
    grad_mixed = jnp.einsum(
        "td,ed->te", grad_attn, full_output, preferred_element_type=jnp.float32
    ).astype(jnp.bfloat16)
    grad_query_rows, grad_keys_all, grad_values_all = attend_backward(
        query_heads, keys_all, values_all, own_ranks, key_ranks, mixed, log_total, grad_mixed
    )
    pair_grads = jnp.concatenate([grad_keys_all, grad_values_all], axis=1).astype(jnp.bfloat16)
    pair_grads = pair_grads.reshape(ctx_count, rows, 2 * kv_width)
    pair_own = jnp.concatenate(reduce_all(thirds(pair_grads), ctx_bits, 3), axis=-1)
    grad_keys_own, grad_values_own = pair_own[:, :kv_width], pair_own[:, kv_width:]
    query_back = rotate(grad_query_rows, cos_part, -sin_part, HEADS).astype(jnp.bfloat16)
    keys_turned = rotate(grad_keys_own, cos_part, -sin_part, KV_HEADS).astype(jnp.bfloat16)
    values_turned = grad_values_own.astype(jnp.bfloat16)
    grad_query = jnp.einsum("td,te->de", act_one, query_back, preferred_element_type=jnp.float32)
    grad_key = jnp.einsum("td,te->de", act_one, keys_turned, preferred_element_type=jnp.float32)
    grad_value = jnp.einsum("td,te->de", act_one, values_turned, preferred_element_type=jnp.float32)
    grad_act_one = jnp.einsum(
        "te,de->td", query_back, full_query, preferred_element_type=jnp.float32
    )
    grad_act_one = grad_act_one + jnp.einsum(
        "te,de->td", keys_turned, full_key, preferred_element_type=jnp.float32
    )
    grad_act_one = grad_act_one + jnp.einsum(
        "te,de->td", values_turned, full_value, preferred_element_type=jnp.float32
    )
    grad_input_norm, grad_gain_one = norm_back(grad_act_one, unit_one, inverse_one, gain_one)
    input_grad = (grad_resid + grad_input_norm).astype(jnp.bfloat16)[None]
    gain_grads = jnp.stack([grad_gain_one, grad_gain_two], axis=0)

    def split_columns(grad):
        return jnp.transpose(
            grad.astype(jnp.bfloat16).reshape(dp_count, depth, ctx_count, -1), (0, 2, 1, 3)
        )

    def as_blocks(blocks, block_rows):
        return pad_rows(blocks, block_rows).reshape(-1, block_rows, width)

    down_blocks = (
        grad_down.astype(jnp.bfloat16)
        .reshape(ctx_count, fold, depth, dp_count, -1)
        .transpose(3, 0, 2, 1, 4)
        .reshape(dp_count, ctx_count, depth, width)
    )
    late_own = reduce_all(
        [
            as_blocks(b, late_rows)
            for b in (split_columns(grad_gate), split_columns(grad_up), down_blocks)
        ],
        all_bits,
        4,
    )
    gain_blocks = jnp.transpose(
        gain_grads.astype(jnp.bfloat16).reshape(2, dp_count, depth), (1, 0, 2)
    )
    gain_blocks = jnp.broadcast_to(gain_blocks[:, None], (dp_count, ctx_count, 2, depth))
    gain_blocks = jnp.pad(gain_blocks, ((0, 0), (0, 0), (0, 0), (0, width - depth)))
    early_blocks = jnp.concatenate(
        [split_columns(g) for g in (grad_query, grad_key, grad_value, grad_output)], axis=-1
    )
    early_blocks = as_blocks(jnp.concatenate([early_blocks, gain_blocks], axis=2), early_rows)
    early_own = jnp.concatenate(reduce_all(thirds(early_blocks), all_bits, 5), axis=-1)
    own_query, own_key, own_value, own_output = (
        early_own[:depth, offsets[n] : offsets[n + 1]] for n in range(4)
    )
    own_gains = early_own[depth : depth + 2, :depth]
    own_down = (
        late_own[2][:depth].reshape(depth, fold, -1).transpose(1, 0, 2).reshape(fold * depth, -1).T
    )
    return (
        outputs,
        input_grad,
        own_gains,
        own_query,
        own_key,
        own_value,
        own_output,
        late_own[0][:depth],
        late_own[1][:depth],
        own_down,
    )


def solution(mesh):
    return jax.shard_map(
        per_device,
        mesh=mesh,
        in_specs=(
            P("dp", "ctx", None),
            P("dp", "ctx", None),
            P("dp", "ctx"),
            P(),
            P(None, "dp"),
            P("dp", "ctx"),
            P("dp", "ctx"),
            P("dp", "ctx"),
            P("dp", "ctx"),
            P("dp", "ctx"),
            P("dp", "ctx"),
            P("dp", "ctx"),
        ),
        out_specs=(
            P("dp", "ctx", None),
            P("dp", "ctx", None),
            P(None, "dp"),
            P("dp", "ctx"),
            P("dp", "ctx"),
            P("dp", "ctx"),
            P("dp", "ctx"),
            P("dp", "ctx"),
            P("dp", "ctx"),
            P("dp", "ctx"),
        ),
        check_vma=False,
    )
```

```python
import functools
import math

import jax
import jax.numpy as jnp
from jax import lax
from jax.experimental import pallas as pl
from jax.experimental.pallas import tpu as pltpu
from jax.sharding import PartitionSpec as P

HEADS = 9
KV_HEADS = 3
HEAD = 64


norm_eps = 1e-05
rope_base = 100000.0
masked_score = -1e30


def normalize(values, gain, size):
    mean = jnp.sum(values * values, axis=-1, keepdims=True) / size
    inverse_rms = lax.rsqrt(mean + norm_eps)
    unit_rows = values * inverse_rms
    return (unit_rows * gain, unit_rows, inverse_rms)


def norm_back(grad, unit_rows, inverse_rms, gain, size):
    grad_unit = grad * gain
    inner = jnp.sum(grad_unit * unit_rows, axis=-1, keepdims=True) / size
    return (inverse_rms * (grad_unit - unit_rows * inner), jnp.sum(grad * unit_rows, axis=0))


def angles_for(positions):
    half_width = HEAD // 2
    inverse = rope_base ** (-(jnp.arange(half_width, dtype=jnp.float32) * 2.0) / HEAD)
    turned = positions.astype(jnp.float32)[:, None] * inverse[None, :]
    return (jnp.cos(turned), jnp.sin(turned))


def rotate(values, cos_part, sin_part, heads):
    shaped = values.reshape(values.shape[0], heads, HEAD)
    front_half = shaped[..., : HEAD // 2]
    back_half = shaped[..., HEAD // 2 :]
    cosine_rows = cos_part[:, None, :]
    sine_rows = sin_part[:, None, :]
    turned = jnp.concatenate(
        [
            front_half * cosine_rows - back_half * sine_rows,
            back_half * cosine_rows + front_half * sine_rows,
        ],
        axis=-1,
    )
    return turned.reshape(values.shape)


def attend_forward_kernel(q_ref, k_ref, v_ref, own_ref, ranks_ref, o_ref, log_ref, kept):
    rows = q_ref.shape[1]
    query = q_ref[0]
    own = own_ref[...]
    count = k_ref.shape[1]

    def score(part, top):
        scores = lax.dot_general(
            query, k_ref[0, part], (((1,), (1,)), ((), ())), preferred_element_type=jnp.float32
        )
        scores = jnp.where(ranks_ref[part] <= own, scores, masked_score)
        kept[part] = scores
        return jnp.maximum(top, jnp.max(scores, axis=1, keepdims=True))

    top = lax.fori_loop(0, count, score, jnp.full((rows, 1), masked_score, jnp.float32))

    def mix(part, carry):
        total, acc = carry
        weights = jnp.exp(kept[part] - top)
        acc = acc + jnp.dot(
            weights.astype(jnp.bfloat16), v_ref[0, part], preferred_element_type=jnp.float32
        )
        return total + jnp.sum(weights, axis=1, keepdims=True), acc

    start = (jnp.zeros((rows, 1), jnp.float32), jnp.zeros((rows, HEAD), jnp.float32))
    total, acc = lax.fori_loop(0, count, mix, start)
    o_ref[0] = (acc / total).astype(jnp.bfloat16)
    log_ref[0] = top + jnp.log(total)


def attend_backward_kernel(
    q_ref, k_ref, v_ref, g_ref, log_ref, inner_ref, own_ref, ranks_ref, dq_ref, dk_ref, dv_ref
):
    rows = q_ref.shape[1]
    query, grad = q_ref[0], g_ref[0]
    own, log_total, inner = own_ref[...], log_ref[0], inner_ref[0]
    across = (((1,), (1,)), ((), ()))

    @pl.when(lax.rem(pl.program_id(0), HEADS // KV_HEADS) == 0)
    def clear():
        dk_ref[...] = jnp.zeros_like(dk_ref)
        dv_ref[...] = jnp.zeros_like(dv_ref)

    def step(part, acc):
        keys = k_ref[0, part]
        scores = lax.dot_general(keys, query, across, preferred_element_type=jnp.float32)
        scores = jnp.where(ranks_ref[part] <= own, scores, masked_score)
        probs = jnp.exp(scores - log_total)
        grad_probs = lax.dot_general(
            v_ref[0, part], grad, across, preferred_element_type=jnp.float32
        )
        grad_scores = (probs * (grad_probs - inner)).astype(jnp.bfloat16)
        dv_ref[0, part] += jnp.dot(
            probs.astype(jnp.bfloat16), grad, preferred_element_type=jnp.float32
        )
        dk_ref[0, part] += jnp.dot(grad_scores, query, preferred_element_type=jnp.float32)
        return acc + lax.dot_general(
            grad_scores, keys, (((0,), (0,)), ((), ())), preferred_element_type=jnp.float32
        )

    acc = lax.fori_loop(0, k_ref.shape[1], step, jnp.zeros((rows, HEAD), jnp.float32))
    dq_ref[0] = acc * (1.0 / math.sqrt(HEAD))


def per_head(shape):
    return pl.BlockSpec((1,) + shape, lambda h: (h,) + (0,) * len(shape))


def per_group(shape):
    return pl.BlockSpec((1,) + shape, lambda h: (h // (HEADS // KV_HEADS),) + (0,) * len(shape))


def shared(shape):
    return pl.BlockSpec(shape, lambda h: (0,) * len(shape))


def attend_forward(query, keys, values, own_ranks, key_ranks, late, bits):
    rows = query.shape[1]
    parts = keys.shape[1]
    mixed, log_total = pl.pallas_call(
        attend_forward_kernel,
        grid=(HEADS,),
        out_shape=[
            jax.ShapeDtypeStruct((HEADS, rows, HEAD), jnp.bfloat16),
            jax.ShapeDtypeStruct((HEADS, rows, 1), jnp.float32),
        ],
        in_specs=[
            per_head((rows, HEAD)),
            per_group((parts, rows, HEAD)),
            per_group((parts, rows, HEAD)),
            shared((rows, 1)),
            shared((parts, 1, rows)),
        ],
        out_specs=[per_head((rows, HEAD)), per_head((rows, 1))],
        scratch_shapes=[pltpu.VMEM((parts, rows, rows), jnp.float32)],
        compiler_params=pltpu.CompilerParams(vmem_limit_bytes=32 << 20),
    )(query, keys, values, own_ranks[:, None], key_ranks.reshape(parts, 1, rows))
    return mixed, log_total, gather_all(late, bits, 1)


def attend_backward(
    query, keys, values, own_ranks, key_ranks, grad, log_total, inner, late, bits
):
    rows = query.shape[1]
    parts = keys.shape[1]
    grads = pl.pallas_call(
        attend_backward_kernel,
        grid=(HEADS,),
        out_shape=[
            jax.ShapeDtypeStruct((HEADS, rows, HEAD), jnp.float32),
            jax.ShapeDtypeStruct((KV_HEADS, parts, rows, HEAD), jnp.float32),
            jax.ShapeDtypeStruct((KV_HEADS, parts, rows, HEAD), jnp.float32),
        ],
        in_specs=[
            per_head((rows, HEAD)),
            per_group((parts, rows, HEAD)),
            per_group((parts, rows, HEAD)),
            per_head((rows, HEAD)),
            per_head((1, rows)),
            per_head((1, rows)),
            shared((1, rows)),
            shared((parts, rows, 1)),
        ],
        out_specs=[
            per_head((rows, HEAD)),
            per_group((parts, rows, HEAD)),
            per_group((parts, rows, HEAD)),
        ],
        compiler_params=pltpu.CompilerParams(vmem_limit_bytes=40 << 20),
    )(
        query,
        keys,
        values,
        grad,
        log_total.reshape(HEADS, 1, rows),
        inner.reshape(HEADS, 1, rows),
        own_ranks[None, :],
        key_ranks.reshape(parts, rows, 1),
    )
    return (*grads, reduce_all(late, bits, 4))


def bit_orders(bits, slices):
    rest = list(bits[1:])
    orders = [
        [bits[0]] + rest,
        [bits[0]] + rest[2:] + rest[:2],
        [bits[0]] + rest[:2][::-1] + rest[2:],
    ]
    return [orders[s % 3] for s in range(slices)]


def bit_values(bits):
    ctx_bits = lax.axis_size("ctx").bit_length() - 1
    dp_index, ctx_index = lax.axis_index("dp"), lax.axis_index("ctx")
    values = {}
    partners = {}
    for bit in bits:
        if bit < ctx_bits:
            step = 1 << bit
            value = lax.rem(ctx_index // step, 2)
            partners[bit] = (dp_index, ctx_index + step * (1 - 2 * value))
        else:
            step = 1 << (bit - ctx_bits)
            value = lax.rem(dp_index // step, 2)
            partners[bit] = (dp_index + step * (1 - 2 * value), ctx_index)
        values[bit] = value
    return values, partners


def greet(partners):
    barrier = pltpu.get_barrier_semaphore()
    for partner in partners.values():
        pl.semaphore_signal(
            barrier, inc=1, device_id=partner, device_id_type=pl.DeviceIdType.MESH
        )
    pl.semaphore_wait(barrier, len(partners))


def gather_body(bits, orders, in_refs, out_refs, local_sem, send_sem, recv_sem):
    values, partners = bit_values(bits)
    stages = len(bits)
    linear = []
    for order in orders:
        total = 0
        for place, bit in enumerate(order):
            total = total + values[bit] * (1 << (stages - 1 - place))
        linear.append(total)
    local = [
        pltpu.make_async_copy(in_refs[s], out_refs[s].at[linear[s]], local_sem.at[s])
        for s in range(len(orders))
    ]
    for copy in local:
        copy.start()
    greet(partners)
    for copy in local:
        copy.wait()
    copies = {}
    for stage in range(stages):
        count = 1 << stage
        for s, order in enumerate(orders):
            if stage > 0:
                copies[s, stage - 1].wait_recv()
            part = out_refs[s].at[pl.ds((linear[s] // count) * count, count)]
            copies[s, stage] = pltpu.make_async_remote_copy(
                src_ref=part,
                dst_ref=part,
                send_sem=send_sem.at[s, stage],
                recv_sem=recv_sem.at[s, stage],
                device_id=partners[order[stages - 1 - stage]],
                device_id_type=pl.DeviceIdType.MESH,
            )
            copies[s, stage].start()
    for s in range(len(orders)):
        copies[s, stages - 1].wait_recv()
        for stage in range(stages):
            copies[s, stage].wait_send()


def gather_kernel(bits, orders, *refs):
    count = len(orders)
    gather_body(bits, orders, refs[:count], refs[count : 2 * count], *refs[2 * count :])


def comm_params(ident, need):
    return pltpu.CompilerParams(
        collective_id=ident, has_side_effects=True, vmem_limit_bytes=need
    )


def standard(order, bits):
    return [order.index(bit) for bit in bits[::-1]]


def gather_all(parts, bits, ident):
    orders = bit_orders(bits, len(parts))
    stages = len(bits)
    total = 1 << stages
    outs = pl.pallas_call(
        functools.partial(gather_kernel, bits, orders),
        out_shape=[jax.ShapeDtypeStruct((total,) + p.shape, p.dtype) for p in parts],
        in_specs=[pl.BlockSpec(memory_space=pltpu.VMEM)] * len(parts),
        out_specs=[pl.BlockSpec(memory_space=pltpu.VMEM)] * len(parts),
        scratch_shapes=[
            pltpu.SemaphoreType.DMA((len(parts),)),
            pltpu.SemaphoreType.DMA((len(parts), stages)),
            pltpu.SemaphoreType.DMA((len(parts), stages)),
        ],
        compiler_params=comm_params(ident, 40 << 20),
    )(*parts)
    results = []
    for out, order in zip(outs, orders):
        shape = out.shape[1:]
        spread = out.reshape((2,) * stages + shape)
        perm = standard(order, bits) + [stages, stages + 1]
        results.append(jnp.transpose(spread, perm).reshape((total,) + shape))
    return results


def reduce_kernel(bits, orders, *refs):
    slices = len(orders)
    stages = len(bits)
    in_refs, out_refs = refs[:slices], refs[slices : 2 * slices]
    recv = refs[2 * slices : 2 * slices + slices * stages]
    work = refs[2 * slices + slices * stages : 2 * slices + slices * (2 * stages - 1)]
    send_sem, recv_sem = refs[-2], refs[-1]
    values, partners = bit_values(bits)
    greet(partners)
    copies = {}
    for stage in range(stages + 1):
        for s, order in enumerate(orders):
            if stage > 0:
                past = stage - 1
                half = 1 << (stages - 1 - past)
                source = in_refs[s] if past == 0 else work[s * (stages - 1) + past - 1]
                arrived = recv[s * stages + past]
                own = values[order[past]] * half
                copies[s, past].wait_recv()
                last = past == stages - 1

                def add(k, unused, source=source, arrived=arrived, own=own, last=last, s=s, past=past):
                    total = source[own + k].astype(jnp.float32) + arrived[k].astype(jnp.float32)
                    if last:
                        out_refs[s][...] = total
                    else:
                        work[s * (stages - 1) + past][k] = total.astype(jnp.bfloat16)
                    return unused

                if last:
                    add(0, 0)
                else:
                    lax.fori_loop(0, half, add, 0)
            if stage < stages:
                half = 1 << (stages - 1 - stage)
                source = in_refs[s] if stage == 0 else work[s * (stages - 1) + stage - 1]
                other = (1 - values[order[stage]]) * half
                copies[s, stage] = pltpu.make_async_remote_copy(
                    src_ref=source.at[pl.ds(other, half)],
                    dst_ref=recv[s * stages + stage],
                    send_sem=send_sem.at[s, stage],
                    recv_sem=recv_sem.at[s, stage],
                    device_id=partners[order[stage]],
                    device_id_type=pl.DeviceIdType.MESH,
                )
                copies[s, stage].start()
    for copy in copies.values():
        copy.wait_send()


def reduce_all(parts, bits, ident):
    orders = bit_orders(bits, len(parts))
    stages = len(bits)
    total = 1 << stages
    ready = []
    for part, order in zip(parts, orders):
        shape = part.shape[1:]
        spread = part.reshape((2,) * stages + shape)
        perm = [stages - 1 - bits.index(bit) for bit in order] + [stages, stages + 1]
        ready.append(jnp.transpose(spread, perm).reshape((total,) + shape))
    recv = [
        pltpu.VMEM((1 << (stages - 1 - t),) + p.shape[1:], jnp.bfloat16)
        for p in parts
        for t in range(stages)
    ]
    work = [
        pltpu.VMEM((1 << (stages - 1 - t),) + p.shape[1:], jnp.bfloat16)
        for p in parts
        for t in range(stages - 1)
    ]
    return pl.pallas_call(
        functools.partial(reduce_kernel, bits, orders),
        out_shape=[jax.ShapeDtypeStruct(p.shape[1:], jnp.float32) for p in parts],
        in_specs=[pl.BlockSpec(memory_space=pltpu.VMEM)] * len(parts),
        out_specs=[pl.BlockSpec(memory_space=pltpu.VMEM)] * len(parts),
        scratch_shapes=recv
        + work
        + [
            pltpu.SemaphoreType.DMA((len(parts), stages)),
            pltpu.SemaphoreType.DMA((len(parts), stages)),
        ],
        compiler_params=comm_params(ident, 56 << 20),
    )(*ready)


def pad_rows(block, rows):
    return jnp.pad(block, ((0, 0),) * (block.ndim - 2) + ((0, rows - block.shape[-2]), (0, 0)))


def thirds(block):
    size = block.shape[-1] // 3
    return [block[..., s * size : (s + 1) * size] for s in range(3)]


def per_device(
    tokens,
    cotangent,
    positions,
    block_order,
    norm_gains,
    w_query,
    w_key,
    w_value,
    w_output,
    w_gate,
    w_up,
    w_down,
):
    ctx_count = lax.axis_size("ctx")
    dp_count = lax.axis_size("dp")
    ctx_bits = list(range(ctx_count.bit_length() - 1))
    all_bits = list(range((ctx_count * dp_count).bit_length() - 1))
    depth = w_query.shape[0]
    size = depth * dp_count
    spans = [w.shape[1] for w in (w_query, w_key, w_value, w_output)]
    offsets = [sum(spans[:n]) for n in range(5)]
    width = sum(spans)
    fold = w_down.shape[1] // depth
    block_rows = -(-(depth + 2) // 16) * 16
    padded = block_rows * dp_count

    def fold_shard(shard):
        blocks = shard.T.reshape(fold, depth, shard.shape[0])
        return blocks.transpose(1, 0, 2).reshape(depth, fold * shard.shape[0])

    def unfold_shard(block):
        blocks = block[:depth].reshape(depth, fold, -1).transpose(1, 0, 2)
        return blocks.reshape(fold * depth, -1).T

    gain_rows = jnp.pad(norm_gains, ((0, block_rows - depth - 2), (0, width - depth)))
    early = jnp.concatenate([w_query, w_key, w_value, fold_shard(w_output)], axis=1)
    early = jnp.concatenate([early, gain_rows], axis=0)
    late = [pad_rows(w, block_rows) for w in (w_gate, w_up, fold_shard(w_down))]
    early_all = jnp.concatenate(gather_all(thirds(early), all_bits, 0), axis=-1)
    early_all = early_all.reshape(dp_count, ctx_count, block_rows, width)

    def join_columns(blocks):
        blocks = blocks.reshape(dp_count, ctx_count, block_rows, -1)
        return jnp.transpose(blocks, (0, 2, 1, 3)).reshape(padded, -1)

    def join_folded(blocks):
        blocks = blocks.reshape(dp_count, ctx_count, block_rows, fold, -1)
        return jnp.transpose(blocks, (1, 3, 2, 0, 4)).reshape(padded, -1)

    def split_columns(grad):
        blocks = grad.astype(jnp.bfloat16).reshape(dp_count, block_rows, ctx_count, -1)
        return jnp.transpose(blocks, (0, 2, 1, 3))

    def split_folded(grad):
        blocks = grad.astype(jnp.bfloat16).reshape(ctx_count, fold, block_rows, dp_count, -1)
        blocks = jnp.transpose(blocks, (3, 0, 2, 1, 4))
        return blocks.reshape(dp_count, ctx_count, block_rows, -1)

    def flat_blocks(blocks):
        return blocks.reshape(dp_count * ctx_count, block_rows, -1)

    def pad_width(values):
        blocks = values.reshape(-1, dp_count, depth)
        blocks = jnp.pad(blocks, ((0, 0), (0, 0), (0, block_rows - depth)))
        return blocks.reshape(-1, padded)

    def cut_width(values):
        return values.reshape(-1, dp_count, block_rows)[:, :, :depth].reshape(-1, size)

    full_query, full_key, full_value = (
        join_columns(early_all[..., offsets[n] : offsets[n + 1]]) for n in range(3)
    )
    output_turned = join_folded(early_all[..., offsets[3] :])
    gains_all = jnp.transpose(early_all[:, 0, depth : depth + 2, :depth], (1, 0, 2))
    gains_all = pad_width(gains_all).astype(jnp.float32)

    rows = tokens.shape[1]
    device_index = lax.axis_index("ctx")
    row_index = jnp.arange(rows, dtype=jnp.int32)
    own_ranks = block_order[device_index] * rows + row_index
    key_ranks = (block_order[:, None] * rows + row_index[None, :]).reshape(-1)
    x_rows = pad_width(tokens[0]).astype(jnp.float32)
    grad_branch = pad_width(cotangent[0])
    grad_out = grad_branch.astype(jnp.float32)
    cos_part, sin_part = angles_for(positions[0])
    gain_one, gain_two = gains_all[0], gains_all[1]
    normed_one, unit_one, inverse_one = normalize(x_rows, gain_one, size)
    act_one = normed_one.astype(jnp.bfloat16)
    query = rotate(
        jnp.dot(act_one, full_query, preferred_element_type=jnp.float32), cos_part, sin_part, HEADS
    ).astype(jnp.bfloat16)
    keys_local = rotate(
        jnp.dot(act_one, full_key, preferred_element_type=jnp.float32), cos_part, sin_part, KV_HEADS
    ).astype(jnp.bfloat16)
    values_local = jnp.dot(act_one, full_value, preferred_element_type=jnp.float32).astype(
        jnp.bfloat16
    )

    def head_major(values):
        return jnp.transpose(values.reshape(rows, HEADS, HEAD), (1, 0, 2))

    def token_major(values):
        return jnp.transpose(values, (1, 0, 2)).reshape(rows, HEADS * HEAD)

    pairs = gather_all(thirds(jnp.concatenate([keys_local, values_local], axis=1)), ctx_bits, 2)
    pairs = jnp.concatenate(pairs, axis=-1).reshape(ctx_count, rows, 2 * KV_HEADS, HEAD)
    pairs = jnp.transpose(pairs, (2, 0, 1, 3))
    keys_all, values_all = pairs[:KV_HEADS], pairs[KV_HEADS:]
    query_heads = head_major(query * jnp.bfloat16(1.0 / math.sqrt(HEAD)))
    mixed, log_total, late_all = attend_forward(
        query_heads, keys_all, values_all, own_ranks, key_ranks, late, all_bits
    )
    mixed_rows = token_major(mixed)
    full_gate, full_up = join_columns(late_all[0]), join_columns(late_all[1])
    down_turned = join_folded(late_all[2])
    resid = x_rows + jnp.einsum(
        "te,de->td", mixed_rows, output_turned, preferred_element_type=jnp.float32
    )
    normed_two, unit_two, inverse_two = normalize(resid, gain_two, size)
    act_two = normed_two.astype(jnp.bfloat16)
    gate = jnp.dot(act_two, full_gate, preferred_element_type=jnp.float32)
    upper = jnp.dot(act_two, full_up, preferred_element_type=jnp.float32)
    sigma = jax.nn.sigmoid(gate)
    hidden = (gate * sigma * upper).astype(jnp.bfloat16)
    result = resid + jnp.einsum(
        "tf,df->td", hidden, down_turned, preferred_element_type=jnp.float32
    )
    outputs = cut_width(result.astype(jnp.bfloat16))[None]
    grad_down = jnp.einsum("td,tf->df", grad_branch, hidden, preferred_element_type=jnp.float32)
    grad_hidden = jnp.dot(grad_branch, down_turned, preferred_element_type=jnp.float32)
    grad_gate_rows = (grad_hidden * upper * sigma * (1.0 + gate * (1.0 - sigma))).astype(
        jnp.bfloat16
    )
    grad_up_rows = (grad_hidden * gate * sigma).astype(jnp.bfloat16)
    grad_gate = jnp.einsum("td,tf->df", act_two, grad_gate_rows, preferred_element_type=jnp.float32)
    grad_up = jnp.einsum("td,tf->df", act_two, grad_up_rows, preferred_element_type=jnp.float32)
    grad_act_two = jnp.einsum(
        "tf,df->td", grad_gate_rows, full_gate, preferred_element_type=jnp.float32
    ) + jnp.einsum("tf,df->td", grad_up_rows, full_up, preferred_element_type=jnp.float32)
    grad_resid_norm, grad_gain_two = norm_back(grad_act_two, unit_two, inverse_two, gain_two, size)
    grad_resid = grad_out + grad_resid_norm
    grad_attn = grad_resid.astype(jnp.bfloat16)
    grad_output = jnp.einsum("td,te->de", grad_attn, mixed_rows, preferred_element_type=jnp.float32)
    grad_mixed = jnp.dot(grad_attn, output_turned, preferred_element_type=jnp.float32).astype(
        jnp.bfloat16
    )
    grad_heads = head_major(grad_mixed)
    inner = jnp.sum(grad_heads.astype(jnp.float32) * mixed.astype(jnp.float32), axis=-1)
    late_blocks = [
        flat_blocks(b)
        for b in (split_columns(grad_gate), split_columns(grad_up), split_folded(grad_down))
    ]
    grad_query_heads, grad_keys_all, grad_values_all, late_own = attend_backward(
        query_heads,
        keys_all,
        values_all,
        own_ranks,
        key_ranks,
        grad_heads,
        log_total,
        inner,
        late_blocks,
        all_bits,
    )
    kv_width = KV_HEADS * HEAD
    pair_grads = jnp.concatenate([grad_keys_all, grad_values_all], axis=0).astype(jnp.bfloat16)
    pair_grads = jnp.transpose(pair_grads, (1, 2, 0, 3)).reshape(ctx_count, rows, 2 * kv_width)
    pair_own = jnp.concatenate(reduce_all(thirds(pair_grads), ctx_bits, 3), axis=-1)
    grad_keys_own, grad_values_own = pair_own[:, :kv_width], pair_own[:, kv_width:]
    query_back = rotate(token_major(grad_query_heads), cos_part, -sin_part, HEADS).astype(
        jnp.bfloat16
    )
    keys_turned = rotate(grad_keys_own, cos_part, -sin_part, KV_HEADS).astype(jnp.bfloat16)
    values_turned = grad_values_own.astype(jnp.bfloat16)
    back_rows = jnp.concatenate([query_back, keys_turned, values_turned], axis=1)
    grad_projections = jnp.einsum(
        "td,te->de", act_one, back_rows, preferred_element_type=jnp.float32
    )
    projections = jnp.concatenate([full_query, full_key, full_value], axis=1)
    grad_act_one = jnp.einsum("te,de->td", back_rows, projections, preferred_element_type=jnp.float32)
    grad_input_norm, grad_gain_one = norm_back(grad_act_one, unit_one, inverse_one, gain_one, size)
    input_grad = cut_width((grad_resid + grad_input_norm).astype(jnp.bfloat16))[None]
    gain_grads = cut_width(jnp.stack([grad_gain_one, grad_gain_two], axis=0))
    gain_blocks = jnp.transpose(
        gain_grads.astype(jnp.bfloat16).reshape(2, dp_count, depth), (1, 0, 2)
    )
    gain_blocks = jnp.pad(
        gain_blocks, ((0, 0), (depth, block_rows - depth - 2), (0, spans[0] - depth))
    )
    query_end, key_end = HEADS * HEAD, HEADS * HEAD + kv_width
    early_blocks = jnp.concatenate(
        [
            split_columns(grad_projections[:, :query_end]) + gain_blocks[:, None],
            split_columns(grad_projections[:, query_end:key_end]),
            split_columns(grad_projections[:, key_end:]),
            split_folded(grad_output),
        ],
        axis=-1,
    )
    early_own = jnp.concatenate(
        reduce_all(thirds(flat_blocks(early_blocks)), all_bits, 5), axis=-1
    )
    own_query, own_key, own_value = (
        early_own[:depth, offsets[n] : offsets[n + 1]] for n in range(3)
    )
    return (
        outputs,
        input_grad,
        early_own[depth : depth + 2, :depth],
        own_query,
        own_key,
        own_value,
        unfold_shard(early_own[:, offsets[3] :]),
        late_own[0][:depth],
        late_own[1][:depth],
        unfold_shard(late_own[2]),
    )


def solution(mesh):
    return jax.shard_map(
        per_device,
        mesh=mesh,
        in_specs=(
            P("dp", "ctx", None),
            P("dp", "ctx", None),
            P("dp", "ctx"),
            P(),
            P(None, "dp"),
            P("dp", "ctx"),
            P("dp", "ctx"),
            P("dp", "ctx"),
            P("dp", "ctx"),
            P("dp", "ctx"),
            P("dp", "ctx"),
            P("dp", "ctx"),
        ),
        out_specs=(
            P("dp", "ctx", None),
            P("dp", "ctx", None),
            P(None, "dp"),
            P("dp", "ctx"),
            P("dp", "ctx"),
            P("dp", "ctx"),
            P("dp", "ctx"),
            P("dp", "ctx"),
            P("dp", "ctx"),
            P("dp", "ctx"),
        ),
        check_vma=False,
    )
```

```python
import functools
import math

import jax
import jax.numpy as jnp
from jax import lax
from jax.experimental import pallas as pl
from jax.experimental.pallas import tpu as pltpu
from jax.sharding import PartitionSpec as P

HEADS = 9
KV_HEADS = 3
HEAD = 64


norm_eps = 1e-05
rope_base = 100000.0
masked_score = -1e30


def normalize(values, gain, size):
    mean = jnp.sum(values * values, axis=-1, keepdims=True) / size
    inverse_rms = lax.rsqrt(mean + norm_eps)
    unit_rows = values * inverse_rms
    return (unit_rows * gain, unit_rows, inverse_rms)


def norm_back(grad, unit_rows, inverse_rms, gain, size):
    grad_unit = grad * gain
    inner = jnp.sum(grad_unit * unit_rows, axis=-1, keepdims=True) / size
    return (inverse_rms * (grad_unit - unit_rows * inner), jnp.sum(grad * unit_rows, axis=0))


def angles_for(positions):
    half_width = HEAD // 2
    inverse = rope_base ** (-(jnp.arange(half_width, dtype=jnp.float32) * 2.0) / HEAD)
    turned = positions.astype(jnp.float32)[:, None] * inverse[None, :]
    return (jnp.cos(turned), jnp.sin(turned))


def rotate(values, cos_part, sin_part, heads):
    shaped = values.reshape(values.shape[0], heads, HEAD)
    front_half = shaped[..., : HEAD // 2]
    back_half = shaped[..., HEAD // 2 :]
    cosine_rows = cos_part[:, None, :]
    sine_rows = sin_part[:, None, :]
    turned = jnp.concatenate(
        [
            front_half * cosine_rows - back_half * sine_rows,
            back_half * cosine_rows + front_half * sine_rows,
        ],
        axis=-1,
    )
    return turned.reshape(values.shape)


def attend_forward_kernel(q_ref, k_ref, v_ref, own_ref, ranks_ref, o_ref, log_ref, kept):
    rows = q_ref.shape[1]
    query = q_ref[0]
    own = own_ref[...]
    count = k_ref.shape[1]

    def score(part, top):
        scores = lax.dot_general(
            query, k_ref[0, part], (((1,), (1,)), ((), ())), preferred_element_type=jnp.float32
        )
        scores = jnp.where(ranks_ref[part] <= own, scores, masked_score)
        kept[part] = scores
        return jnp.maximum(top, jnp.max(scores, axis=1, keepdims=True))

    top = lax.fori_loop(0, count, score, jnp.full((rows, 1), masked_score, jnp.float32))

    def mix(part, carry):
        total, acc = carry
        weights = jnp.exp(kept[part] - top)
        acc = acc + jnp.dot(
            weights.astype(jnp.bfloat16), v_ref[0, part], preferred_element_type=jnp.float32
        )
        return total + jnp.sum(weights, axis=1, keepdims=True), acc

    start = (jnp.zeros((rows, 1), jnp.float32), jnp.zeros((rows, HEAD), jnp.float32))
    total, acc = lax.fori_loop(0, count, mix, start)
    o_ref[0] = (acc / total).astype(jnp.bfloat16)
    log_ref[0] = top + jnp.log(total)


def attend_backward_kernel(
    q_ref, k_ref, v_ref, g_ref, log_ref, inner_ref, own_ref, ranks_ref, dq_ref, dk_ref, dv_ref
):
    rows = q_ref.shape[1]
    query, grad = q_ref[0], g_ref[0]
    own, log_total, inner = own_ref[...], log_ref[0], inner_ref[0]
    across = (((1,), (1,)), ((), ()))

    @pl.when(lax.rem(pl.program_id(0), HEADS // KV_HEADS) == 0)
    def clear():
        dk_ref[...] = jnp.zeros_like(dk_ref)
        dv_ref[...] = jnp.zeros_like(dv_ref)

    def step(part, acc):
        keys = k_ref[0, part]
        scores = lax.dot_general(keys, query, across, preferred_element_type=jnp.float32)
        scores = jnp.where(ranks_ref[part] <= own, scores, masked_score)
        probs = jnp.exp(scores - log_total)
        grad_probs = lax.dot_general(
            v_ref[0, part], grad, across, preferred_element_type=jnp.float32
        )
        grad_scores = (probs * (grad_probs - inner)).astype(jnp.bfloat16)
        dv_ref[0, part] += jnp.dot(
            probs.astype(jnp.bfloat16), grad, preferred_element_type=jnp.float32
        )
        dk_ref[0, part] += jnp.dot(grad_scores, query, preferred_element_type=jnp.float32)
        return acc + lax.dot_general(
            grad_scores, keys, (((0,), (0,)), ((), ())), preferred_element_type=jnp.float32
        )

    acc = lax.fori_loop(0, k_ref.shape[1], step, jnp.zeros((rows, HEAD), jnp.float32))
    dq_ref[0] = acc * (1.0 / math.sqrt(HEAD))


def per_head(shape):
    return pl.BlockSpec((1,) + shape, lambda h: (h,) + (0,) * len(shape))


def per_group(shape):
    return pl.BlockSpec((1,) + shape, lambda h: (h // (HEADS // KV_HEADS),) + (0,) * len(shape))


def shared(shape):
    return pl.BlockSpec(shape, lambda h: (0,) * len(shape))


def attend_forward(query, keys, values, own_ranks, key_ranks, late, bits):
    rows = query.shape[1]
    parts = keys.shape[1]
    mixed, log_total = pl.pallas_call(
        attend_forward_kernel,
        grid=(HEADS,),
        out_shape=[
            jax.ShapeDtypeStruct((HEADS, rows, HEAD), jnp.bfloat16),
            jax.ShapeDtypeStruct((HEADS, rows, 1), jnp.float32),
        ],
        in_specs=[
            per_head((rows, HEAD)),
            per_group((parts, rows, HEAD)),
            per_group((parts, rows, HEAD)),
            shared((rows, 1)),
            shared((parts, 1, rows)),
        ],
        out_specs=[per_head((rows, HEAD)), per_head((rows, 1))],
        scratch_shapes=[pltpu.VMEM((parts, rows, rows), jnp.float32)],
        compiler_params=pltpu.CompilerParams(vmem_limit_bytes=32 << 20),
    )(query, keys, values, own_ranks[:, None], key_ranks.reshape(parts, 1, rows))
    return mixed, log_total, gather_all(late, bits, 1)


def attend_backward(
    query, keys, values, own_ranks, key_ranks, grad, log_total, inner, late, bits
):
    rows = query.shape[1]
    parts = keys.shape[1]
    grads = pl.pallas_call(
        attend_backward_kernel,
        grid=(HEADS,),
        out_shape=[
            jax.ShapeDtypeStruct((HEADS, rows, HEAD), jnp.float32),
            jax.ShapeDtypeStruct((KV_HEADS, parts, rows, HEAD), jnp.float32),
            jax.ShapeDtypeStruct((KV_HEADS, parts, rows, HEAD), jnp.float32),
        ],
        in_specs=[
            per_head((rows, HEAD)),
            per_group((parts, rows, HEAD)),
            per_group((parts, rows, HEAD)),
            per_head((rows, HEAD)),
            per_head((1, rows)),
            per_head((1, rows)),
            shared((1, rows)),
            shared((parts, rows, 1)),
        ],
        out_specs=[
            per_head((rows, HEAD)),
            per_group((parts, rows, HEAD)),
            per_group((parts, rows, HEAD)),
        ],
        compiler_params=pltpu.CompilerParams(vmem_limit_bytes=40 << 20),
    )(
        query,
        keys,
        values,
        grad,
        log_total.reshape(HEADS, 1, rows),
        inner.reshape(HEADS, 1, rows),
        own_ranks[None, :],
        key_ranks.reshape(parts, rows, 1),
    )
    return (*grads, reduce_all(late, bits, 4))


def bit_orders(bits, slices):
    rest = list(bits[1:])
    orders = [
        [bits[0]] + rest,
        [bits[0]] + rest[2:] + rest[:2],
        [bits[0]] + rest[:2][::-1] + rest[2:],
    ]
    return [orders[s % 3] for s in range(slices)]


def bit_values(bits):
    ctx_bits = lax.axis_size("ctx").bit_length() - 1
    dp_index, ctx_index = lax.axis_index("dp"), lax.axis_index("ctx")
    values = {}
    partners = {}
    for bit in bits:
        if bit < ctx_bits:
            step = 1 << bit
            value = lax.rem(ctx_index // step, 2)
            partners[bit] = (dp_index, ctx_index + step * (1 - 2 * value))
        else:
            step = 1 << (bit - ctx_bits)
            value = lax.rem(dp_index // step, 2)
            partners[bit] = (dp_index + step * (1 - 2 * value), ctx_index)
        values[bit] = value
    return values, partners


def greet(partners):
    barrier = pltpu.get_barrier_semaphore()
    for partner in partners.values():
        pl.semaphore_signal(
            barrier, inc=1, device_id=partner, device_id_type=pl.DeviceIdType.MESH
        )
    pl.semaphore_wait(barrier, len(partners))


def gather_body(bits, orders, in_refs, out_refs, local_sem, send_sem, recv_sem):
    values, partners = bit_values(bits)
    stages = len(bits)
    linear = []
    for order in orders:
        total = 0
        for place, bit in enumerate(order):
            total = total + values[bit] * (1 << (stages - 1 - place))
        linear.append(total)
    local = [
        pltpu.make_async_copy(in_refs[s], out_refs[s].at[linear[s]], local_sem.at[s])
        for s in range(len(orders))
    ]
    for copy in local:
        copy.start()
    greet(partners)
    for copy in local:
        copy.wait()
    copies = {}
    for stage in range(stages):
        count = 1 << stage
        for s, order in enumerate(orders):
            if stage > 0:
                copies[s, stage - 1].wait_recv()
            part = out_refs[s].at[pl.ds((linear[s] // count) * count, count)]
            copies[s, stage] = pltpu.make_async_remote_copy(
                src_ref=part,
                dst_ref=part,
                send_sem=send_sem.at[s, stage],
                recv_sem=recv_sem.at[s, stage],
                device_id=partners[order[stages - 1 - stage]],
                device_id_type=pl.DeviceIdType.MESH,
            )
            copies[s, stage].start()
    for s in range(len(orders)):
        copies[s, stages - 1].wait_recv()
        for stage in range(stages):
            copies[s, stage].wait_send()


def gather_kernel(bits, orders, *refs):
    count = len(orders)
    gather_body(bits, orders, refs[:count], refs[count : 2 * count], *refs[2 * count :])


def comm_params(ident, need):
    return pltpu.CompilerParams(
        collective_id=ident, has_side_effects=True, vmem_limit_bytes=need
    )


def standard(order, bits):
    return [order.index(bit) for bit in bits[::-1]]


def gather_all(parts, bits, ident):
    orders = bit_orders(bits, len(parts))
    stages = len(bits)
    total = 1 << stages
    outs = pl.pallas_call(
        functools.partial(gather_kernel, bits, orders),
        out_shape=[jax.ShapeDtypeStruct((total,) + p.shape, p.dtype) for p in parts],
        in_specs=[pl.BlockSpec(memory_space=pltpu.VMEM)] * len(parts),
        out_specs=[pl.BlockSpec(memory_space=pltpu.VMEM)] * len(parts),
        scratch_shapes=[
            pltpu.SemaphoreType.DMA((len(parts),)),
            pltpu.SemaphoreType.DMA((len(parts), stages)),
            pltpu.SemaphoreType.DMA((len(parts), stages)),
        ],
        compiler_params=comm_params(ident, 40 << 20),
    )(*parts)
    results = []
    for out, order in zip(outs, orders):
        shape = out.shape[1:]
        spread = out.reshape((2,) * stages + shape)
        perm = standard(order, bits) + [stages, stages + 1]
        results.append(jnp.transpose(spread, perm).reshape((total,) + shape))
    return results


def reduce_kernel(bits, orders, *refs):
    slices = len(orders)
    stages = len(bits)
    in_refs, out_refs = refs[:slices], refs[slices : 2 * slices]
    recv = refs[2 * slices : 2 * slices + slices * stages]
    work = refs[2 * slices + slices * stages : 2 * slices + slices * (2 * stages - 1)]
    send_sem, recv_sem = refs[-2], refs[-1]
    values, partners = bit_values(bits)
    greet(partners)
    copies = {}
    for stage in range(stages + 1):
        for s, order in enumerate(orders):
            if stage > 0:
                past = stage - 1
                half = 1 << (stages - 1 - past)
                source = in_refs[s] if past == 0 else work[s * (stages - 1) + past - 1]
                arrived = recv[s * stages + past]
                own = values[order[past]] * half
                copies[s, past].wait_recv()
                last = past == stages - 1

                def add(k, unused, source=source, arrived=arrived, own=own, last=last, s=s, past=past):
                    total = source[own + k].astype(jnp.float32) + arrived[k].astype(jnp.float32)
                    if last:
                        out_refs[s][...] = total
                    else:
                        work[s * (stages - 1) + past][k] = total.astype(jnp.bfloat16)
                    return unused

                if last:
                    add(0, 0)
                else:
                    lax.fori_loop(0, half, add, 0)
            if stage < stages:
                half = 1 << (stages - 1 - stage)
                source = in_refs[s] if stage == 0 else work[s * (stages - 1) + stage - 1]
                other = (1 - values[order[stage]]) * half
                copies[s, stage] = pltpu.make_async_remote_copy(
                    src_ref=source.at[pl.ds(other, half)],
                    dst_ref=recv[s * stages + stage],
                    send_sem=send_sem.at[s, stage],
                    recv_sem=recv_sem.at[s, stage],
                    device_id=partners[order[stage]],
                    device_id_type=pl.DeviceIdType.MESH,
                )
                copies[s, stage].start()
    for copy in copies.values():
        copy.wait_send()


def reduce_all(parts, bits, ident):
    orders = bit_orders(bits, len(parts))
    stages = len(bits)
    total = 1 << stages
    ready = []
    for part, order in zip(parts, orders):
        shape = part.shape[1:]
        spread = part.reshape((2,) * stages + shape)
        perm = [stages - 1 - bits.index(bit) for bit in order] + [stages, stages + 1]
        ready.append(jnp.transpose(spread, perm).reshape((total,) + shape))
    recv = [
        pltpu.VMEM((1 << (stages - 1 - t),) + p.shape[1:], jnp.bfloat16)
        for p in parts
        for t in range(stages)
    ]
    work = [
        pltpu.VMEM((1 << (stages - 1 - t),) + p.shape[1:], jnp.bfloat16)
        for p in parts
        for t in range(stages - 1)
    ]
    return pl.pallas_call(
        functools.partial(reduce_kernel, bits, orders),
        out_shape=[jax.ShapeDtypeStruct(p.shape[1:], jnp.float32) for p in parts],
        in_specs=[pl.BlockSpec(memory_space=pltpu.VMEM)] * len(parts),
        out_specs=[pl.BlockSpec(memory_space=pltpu.VMEM)] * len(parts),
        scratch_shapes=recv
        + work
        + [
            pltpu.SemaphoreType.DMA((len(parts), stages)),
            pltpu.SemaphoreType.DMA((len(parts), stages)),
        ],
        compiler_params=comm_params(ident, 56 << 20),
    )(*ready)


def pad_rows(block, rows):
    return jnp.pad(block, ((0, 0),) * (block.ndim - 2) + ((0, rows - block.shape[-2]), (0, 0)))


def thirds(block):
    size = block.shape[-1] // 3
    return [block[..., s * size : (s + 1) * size] for s in range(3)]


def per_device(
    tokens,
    cotangent,
    positions,
    block_order,
    norm_gains,
    w_query,
    w_key,
    w_value,
    w_output,
    w_gate,
    w_up,
    w_down,
):
    ctx_count = lax.axis_size("ctx")
    dp_count = lax.axis_size("dp")
    ctx_bits = list(range(ctx_count.bit_length() - 1))
    all_bits = list(range((ctx_count * dp_count).bit_length() - 1))
    depth = w_query.shape[0]
    size = depth * dp_count
    spans = [w.shape[1] for w in (w_query, w_key, w_value, w_output)]
    offsets = [sum(spans[:n]) for n in range(5)]
    width = sum(spans)
    fold = w_down.shape[1] // depth
    block_rows = -(-(depth + 2) // 16) * 16
    padded = block_rows * dp_count

    def fold_shard(shard):
        blocks = shard.T.reshape(fold, depth, shard.shape[0])
        return blocks.transpose(1, 0, 2).reshape(depth, fold * shard.shape[0])

    def unfold_shard(block):
        blocks = block[:depth].reshape(depth, fold, -1).transpose(1, 0, 2)
        return blocks.reshape(fold * depth, -1).T

    gain_rows = jnp.pad(norm_gains, ((0, block_rows - depth - 2), (0, width - depth)))
    early = jnp.concatenate([w_query, w_key, w_value, fold_shard(w_output)], axis=1)
    early = jnp.concatenate([early, gain_rows], axis=0)
    late = [pad_rows(w, block_rows) for w in (w_gate, w_up, fold_shard(w_down))]
    early_all = jnp.concatenate(gather_all(thirds(early), all_bits, 0), axis=-1)
    early_all = early_all.reshape(dp_count, ctx_count, block_rows, width)

    def join_columns(blocks):
        blocks = blocks.reshape(dp_count, ctx_count, block_rows, -1)
        return jnp.concatenate(
            [blocks[:, j].reshape(padded, -1) for j in range(ctx_count)], axis=1
        )

    def join_folded(blocks):
        blocks = blocks.reshape(dp_count, ctx_count, block_rows, -1)
        span = blocks.shape[-1] // fold
        pieces = [
            jnp.stack(
                [blocks[i, :, :, m * span : (m + 1) * span] for m in range(fold)], axis=1
            ).reshape(padded, span)
            for i in range(dp_count)
        ]
        return jnp.concatenate(pieces, axis=1)

    def split_columns(grad):
        grad = grad.astype(jnp.bfloat16)
        span = grad.shape[1] // ctx_count
        pieces = [
            grad[:, j * span : (j + 1) * span].reshape(dp_count, block_rows, span)
            for j in range(ctx_count)
        ]
        return jnp.stack(pieces, axis=1)

    def split_folded(grad):
        grad = grad.astype(jnp.bfloat16)
        span = grad.shape[1] // dp_count
        pieces = []
        for i in range(dp_count):
            part = grad[:, i * span : (i + 1) * span]
            part = part.reshape(ctx_count, fold, block_rows, span)
            pieces.append(jnp.concatenate([part[:, m] for m in range(fold)], axis=-1))
        return jnp.stack(pieces, axis=0)

    def flat_blocks(blocks):
        return blocks.reshape(dp_count * ctx_count, block_rows, -1)

    def pad_width(values):
        blocks = values.reshape(-1, dp_count, depth)
        blocks = jnp.pad(blocks, ((0, 0), (0, 0), (0, block_rows - depth)))
        return blocks.reshape(-1, padded)

    def cut_width(values):
        return values.reshape(-1, dp_count, block_rows)[:, :, :depth].reshape(-1, size)

    full_query, full_key, full_value = (
        join_columns(early_all[..., offsets[n] : offsets[n + 1]]) for n in range(3)
    )
    output_turned = join_folded(early_all[..., offsets[3] :])
    gains_all = jnp.transpose(early_all[:, 0, depth : depth + 2, :depth], (1, 0, 2))
    gains_all = pad_width(gains_all).astype(jnp.float32)

    rows = tokens.shape[1]
    device_index = lax.axis_index("ctx")
    row_index = jnp.arange(rows, dtype=jnp.int32)
    own_ranks = block_order[device_index] * rows + row_index
    key_ranks = (block_order[:, None] * rows + row_index[None, :]).reshape(-1)
    x_rows = pad_width(tokens[0]).astype(jnp.float32)
    grad_branch = pad_width(cotangent[0])
    grad_out = grad_branch.astype(jnp.float32)
    cos_part, sin_part = angles_for(positions[0])
    gain_one, gain_two = gains_all[0], gains_all[1]
    normed_one, unit_one, inverse_one = normalize(x_rows, gain_one, size)
    act_one = normed_one.astype(jnp.bfloat16)
    query = rotate(
        jnp.dot(act_one, full_query, preferred_element_type=jnp.float32), cos_part, sin_part, HEADS
    ).astype(jnp.bfloat16)
    keys_local = rotate(
        jnp.dot(act_one, full_key, preferred_element_type=jnp.float32), cos_part, sin_part, KV_HEADS
    ).astype(jnp.bfloat16)
    values_local = jnp.dot(act_one, full_value, preferred_element_type=jnp.float32).astype(
        jnp.bfloat16
    )

    def head_major(values):
        return jnp.transpose(values.reshape(rows, HEADS, HEAD), (1, 0, 2))

    def token_major(values):
        return jnp.transpose(values, (1, 0, 2)).reshape(rows, HEADS * HEAD)

    pairs = gather_all(thirds(jnp.concatenate([keys_local, values_local], axis=1)), ctx_bits, 2)
    pairs = jnp.concatenate(pairs, axis=-1).reshape(ctx_count, rows, 2 * KV_HEADS, HEAD)
    pairs = jnp.transpose(pairs, (2, 0, 1, 3))
    keys_all, values_all = pairs[:KV_HEADS], pairs[KV_HEADS:]
    query_heads = head_major(query * jnp.bfloat16(1.0 / math.sqrt(HEAD)))
    mixed, log_total, late_all = attend_forward(
        query_heads, keys_all, values_all, own_ranks, key_ranks, late, all_bits
    )
    mixed_rows = token_major(mixed)
    full_gate, full_up = join_columns(late_all[0]), join_columns(late_all[1])
    down_turned = join_folded(late_all[2])
    resid = x_rows + jnp.einsum(
        "te,de->td", mixed_rows, output_turned, preferred_element_type=jnp.float32
    )
    normed_two, unit_two, inverse_two = normalize(resid, gain_two, size)
    act_two = normed_two.astype(jnp.bfloat16)
    gate = jnp.dot(act_two, full_gate, preferred_element_type=jnp.float32)
    upper = jnp.dot(act_two, full_up, preferred_element_type=jnp.float32)
    sigma = jax.nn.sigmoid(gate)
    hidden = (gate * sigma * upper).astype(jnp.bfloat16)
    result = resid + jnp.einsum(
        "tf,df->td", hidden, down_turned, preferred_element_type=jnp.float32
    )
    outputs = cut_width(result.astype(jnp.bfloat16))[None]
    grad_down = jnp.einsum("td,tf->df", grad_branch, hidden, preferred_element_type=jnp.float32)
    grad_hidden = jnp.dot(grad_branch, down_turned, preferred_element_type=jnp.float32)
    grad_gate_rows = (grad_hidden * upper * sigma * (1.0 + gate * (1.0 - sigma))).astype(
        jnp.bfloat16
    )
    grad_up_rows = (grad_hidden * gate * sigma).astype(jnp.bfloat16)
    grad_gate = jnp.einsum("td,tf->df", act_two, grad_gate_rows, preferred_element_type=jnp.float32)
    grad_up = jnp.einsum("td,tf->df", act_two, grad_up_rows, preferred_element_type=jnp.float32)
    grad_act_two = jnp.einsum(
        "tf,df->td", grad_gate_rows, full_gate, preferred_element_type=jnp.float32
    ) + jnp.einsum("tf,df->td", grad_up_rows, full_up, preferred_element_type=jnp.float32)
    grad_resid_norm, grad_gain_two = norm_back(grad_act_two, unit_two, inverse_two, gain_two, size)
    grad_resid = grad_out + grad_resid_norm
    grad_attn = grad_resid.astype(jnp.bfloat16)
    grad_output = jnp.einsum("td,te->de", grad_attn, mixed_rows, preferred_element_type=jnp.float32)
    grad_mixed = jnp.dot(grad_attn, output_turned, preferred_element_type=jnp.float32).astype(
        jnp.bfloat16
    )
    grad_heads = head_major(grad_mixed)
    inner = jnp.sum(grad_heads.astype(jnp.float32) * mixed.astype(jnp.float32), axis=-1)
    late_blocks = [
        flat_blocks(b)
        for b in (split_columns(grad_gate), split_columns(grad_up), split_folded(grad_down))
    ]
    grad_query_heads, grad_keys_all, grad_values_all, late_own = attend_backward(
        query_heads,
        keys_all,
        values_all,
        own_ranks,
        key_ranks,
        grad_heads,
        log_total,
        inner,
        late_blocks,
        all_bits,
    )
    kv_width = KV_HEADS * HEAD
    pair_grads = jnp.concatenate([grad_keys_all, grad_values_all], axis=0).astype(jnp.bfloat16)
    pair_grads = jnp.transpose(pair_grads, (1, 2, 0, 3)).reshape(ctx_count, rows, 2 * kv_width)
    pair_own = jnp.concatenate(reduce_all(thirds(pair_grads), ctx_bits, 3), axis=-1)
    grad_keys_own, grad_values_own = pair_own[:, :kv_width], pair_own[:, kv_width:]
    query_back = rotate(token_major(grad_query_heads), cos_part, -sin_part, HEADS).astype(
        jnp.bfloat16
    )
    keys_turned = rotate(grad_keys_own, cos_part, -sin_part, KV_HEADS).astype(jnp.bfloat16)
    values_turned = grad_values_own.astype(jnp.bfloat16)
    back_rows = jnp.concatenate([query_back, keys_turned, values_turned], axis=1)
    grad_projections = jnp.einsum(
        "td,te->de", act_one, back_rows, preferred_element_type=jnp.float32
    )
    projections = jnp.concatenate([full_query, full_key, full_value], axis=1)
    grad_act_one = jnp.einsum("te,de->td", back_rows, projections, preferred_element_type=jnp.float32)
    grad_input_norm, grad_gain_one = norm_back(grad_act_one, unit_one, inverse_one, gain_one, size)
    input_grad = cut_width((grad_resid + grad_input_norm).astype(jnp.bfloat16))[None]
    gain_grads = cut_width(jnp.stack([grad_gain_one, grad_gain_two], axis=0))
    gain_blocks = jnp.transpose(
        gain_grads.astype(jnp.bfloat16).reshape(2, dp_count, depth), (1, 0, 2)
    )
    gain_blocks = jnp.pad(
        gain_blocks, ((0, 0), (depth, block_rows - depth - 2), (0, spans[0] - depth))
    )
    query_end, key_end = HEADS * HEAD, HEADS * HEAD + kv_width
    early_blocks = jnp.concatenate(
        [
            split_columns(grad_projections[:, :query_end]) + gain_blocks[:, None],
            split_columns(grad_projections[:, query_end:key_end]),
            split_columns(grad_projections[:, key_end:]),
            split_folded(grad_output),
        ],
        axis=-1,
    )
    early_own = jnp.concatenate(
        reduce_all(thirds(flat_blocks(early_blocks)), all_bits, 5), axis=-1
    )
    own_query, own_key, own_value = (
        early_own[:depth, offsets[n] : offsets[n + 1]] for n in range(3)
    )
    return (
        outputs,
        input_grad,
        early_own[depth : depth + 2, :depth],
        own_query,
        own_key,
        own_value,
        unfold_shard(early_own[:, offsets[3] :]),
        late_own[0][:depth],
        late_own[1][:depth],
        unfold_shard(late_own[2]),
    )


def solution(mesh):
    return jax.shard_map(
        per_device,
        mesh=mesh,
        in_specs=(
            P("dp", "ctx", None),
            P("dp", "ctx", None),
            P("dp", "ctx"),
            P(),
            P(None, "dp"),
            P("dp", "ctx"),
            P("dp", "ctx"),
            P("dp", "ctx"),
            P("dp", "ctx"),
            P("dp", "ctx"),
            P("dp", "ctx"),
            P("dp", "ctx"),
        ),
        out_specs=(
            P("dp", "ctx", None),
            P("dp", "ctx", None),
            P(None, "dp"),
            P("dp", "ctx"),
            P("dp", "ctx"),
            P("dp", "ctx"),
            P("dp", "ctx"),
            P("dp", "ctx"),
            P("dp", "ctx"),
            P("dp", "ctx"),
        ),
        check_vma=False,
    )
```
